32 devices in a mesh: gx: 8 (over y, x, core), gy: 4 (over z).
Axes of the slice: x: 2, y: 2, z: 4, core: 2. Of those that a mesh axis runs over, the one named last changes fastest.
Arguments:
- features: bfloat16 [32768, 256], P(('gx', 'gy')), may hold values from -6 to 6
- valid: int32 [32768], P(('gx', 'gy')), may hold values from 0 to 1, as said below
- cotangent: bfloat16 [32768, 256], P(('gx', 'gy')), may hold values from -6 to 6
- gamma: float32 [256], replicated, may hold values from 0.5 to 1.5
- w_qkv: bfloat16 [256, 768], replicated
- w_out: bfloat16 [256, 256], replicated, may hold values from -0.375 to 0.375
Outputs:
- block_out: bfloat16 [32768, 256], P(('gx', 'gy'))
- grad_x: bfloat16 [32768, 256], P(('gx', 'gy'))
- grad_wqkv: float32 [256, 768], replicated
- grad_wout: float32 [256, 256], replicated
- gamma_gradient: float32 [256], replicated
The draws below stay inside these ranges and needn't reach their ends.
Inputs may be any that keep to these rules, and one draw needn't show every extreme that they name: `valid`: the node that takes the first position of each patch in transposed order is occupied.
All inputs are finite; a program needn't handle non-finite values.
Results may differ from the reference program's by a relative error of at most 0.015.
The reference program's roundings to bfloat16 on the way count: a program that leaves them out, or rounds other values in their place, can miss the bound.
Values may be sent and summed in bfloat16 or wider, within the bound.
A program may use at most 64 MiB of HBM per device.

```python
import jax
import jax.numpy as jnp
from jax import lax

C = 256
HEADS = 16
K = 1024
ROWS = 1024
BLOCK = 32
NODES = 32768
N_GX = 8
N_GY = 4


def draw_valid(key, part):
    count = N_GX * N_GY
    level = jax.random.randint(jax.random.fold_in(key, 11), (count,), 1, 5)
    level = level.at[0].set(4)
    draws = jax.random.randint(jax.random.fold_in(key, 12), (NODES,), 0, 4)
    index = jnp.arange(NODES, dtype=jnp.int32)
    device = index // ROWS
    offset = index % BLOCK
    source = index // BLOCK % count
    target = index // (BLOCK * count)
    moved = (source * count + target) * BLOCK + offset
    first = moved % K == 0
    occupied = jnp.logical_or(draws < level[device], first)
    return jnp.where(occupied, 1, 0).astype(jnp.int32)


def draw_w_qkv(key, part):
    scale = C ** (-0.5)
    full = jax.random.normal(jax.random.fold_in(key, 23), (C, 3 * C), jnp.float32) * scale
    return full.astype(jnp.bfloat16)


def block_levels(own_key, dims, shards, least, high):
    level = 1.0
    for axis_at, blocks in shards:
        heights = jax.random.uniform(jax.random.fold_in(jax.random.fold_in(own_key, 6), axis_at), (blocks,), jnp.float32, least / len(shards), high / len(shards))
        level = level * jnp.repeat(jnp.exp(heights), dims[axis_at] // blocks).reshape((-1,) + (1,) * (len(dims) - 1 - axis_at))
    return level


def centred(own_key, dims, spread, limit, cuts=(), held_as=jnp.bfloat16):
    entries = jax.random.normal(own_key, dims, jnp.float32) * spread
    if len(cuts) > 0:
        entries = block_levels(own_key, dims, cuts, -0.22, 0.18) * entries
    return jnp.clip(entries, min=-limit, max=limit).astype(held_as)


def setup_inputs(seed: int = 0) -> dict:
    splits = jax.random.split(jax.random.key(seed), 7)
    return {
        "features": centred(splits[0], (NODES, C), 1.0, 6.0, ((0, 32),)),
        "valid": draw_valid(jax.random.fold_in(splits[6], 71), 0),
        "cotangent": centred(splits[2], (NODES, C), 1.0, 6.0, ((0, 32),)),
        "gamma": jnp.clip(1.0 + 0.1 * jax.random.normal(splits[3], (C,), jnp.float32), 0.5, 1.5),
        "w_qkv": draw_w_qkv(jax.random.fold_in(splits[6], 71), 0),
        "w_out": centred(splits[5], (C, C), C ** -0.5, 0.375),
    }


def reorder(array, count, block):
    rest = array.shape[1:]
    shaped = array.reshape((count, count, block) + rest)
    return jnp.swapaxes(shaped, 0, 1).reshape(array.shape)

def layer_norm_apply(input_rows, gamma):
    xf = input_rows.astype(jnp.float32)
    centered_input = xf - lax.optimization_barrier(jnp.mean(xf, -1, keepdims=True))
    reciprocal_deviation = lax.rsqrt(lax.optimization_barrier(jnp.mean(centered_input * centered_input, -1, keepdims=True)) + 1e-05)
    normalized_input = centered_input * reciprocal_deviation
    return (normalized_input, reciprocal_deviation, (normalized_input * gamma.astype(jnp.float32)).astype(jnp.bfloat16))

def head_probs(query, keys, keep, scale):
    scores = jnp.dot(query, keys.T, preferred_element_type=jnp.float32) * scale
    scores = jnp.where(keep[None, :], scores, -1e+30)
    expo = jnp.exp(scores - lax.optimization_barrier(jnp.max(scores, -1, keepdims=True)))
    return expo / lax.optimization_barrier(jnp.sum(expo, -1, keepdims=True))

def split_heads(block, heads):
    return block.reshape(block.shape[0], heads, -1).transpose(1, 0, 2)

def join_heads(block):
    return block.transpose(1, 0, 2).reshape(block.shape[1], -1)

def patch_forward(qkv_block, keep, heads):
    width = qkv_block.shape[1] // 3
    scale = (width // heads) ** (-0.5)
    query = split_heads(qkv_block[:, :width], heads)
    keys = split_heads(qkv_block[:, width:2 * width], heads)
    values = split_heads(qkv_block[:, 2 * width:], heads)

    def one_head(parts):
        probs = head_probs(parts[0], parts[1], keep, scale).astype(jnp.bfloat16)
        return jnp.dot(probs, parts[2], preferred_element_type=jnp.float32).astype(jnp.bfloat16)
    return join_heads(lax.map(one_head, (query, keys, values)))

def patch_backward(qkv_block, keep, grad_block, heads):
    width = qkv_block.shape[1] // 3
    scale = (width // heads) ** (-0.5)
    query = split_heads(qkv_block[:, :width], heads)
    keys = split_heads(qkv_block[:, width:2 * width], heads)
    values = split_heads(qkv_block[:, 2 * width:], heads)
    grads = split_heads(grad_block, heads)

    def one_head(parts):
        q_head, k_head, v_head, g_head = parts
        probs = head_probs(q_head, k_head, keep, scale)
        rounded = probs.astype(jnp.bfloat16)
        d_value = jnp.dot(rounded.T, g_head, preferred_element_type=jnp.float32).astype(jnp.bfloat16)
        d_prob = jnp.dot(g_head, v_head.T, preferred_element_type=jnp.float32)
        d_score = (probs * (d_prob - lax.optimization_barrier(jnp.sum(d_prob * probs, -1, keepdims=True))) * scale).astype(jnp.bfloat16)
        d_query = jnp.dot(d_score, k_head, preferred_element_type=jnp.float32).astype(jnp.bfloat16)
        d_key = jnp.dot(d_score.T, q_head, preferred_element_type=jnp.float32).astype(jnp.bfloat16)
        return (d_query, d_key, d_value)
    d_query, d_key, d_value = lax.map(one_head, (query, keys, values, grads))
    return jnp.concatenate([join_heads(d_query), join_heads(d_key), join_heads(d_value)], 1)

def reference(features, valid, cotangent, gamma, w_qkv, w_out):
    count = N_GX * N_GY
    block = NODES // (count * count)
    input_rows = reorder(features, count, block)
    keep = reorder(valid, count, block) > 0
    gt = reorder(cotangent, count, block)
    inverse_root = float(NODES) ** (-0.5)
    normalized_input, reciprocal_deviation, hidden_state = layer_norm_apply(input_rows, gamma)
    qkv = jnp.dot(hidden_state, w_qkv, preferred_element_type=jnp.float32).astype(jnp.bfloat16)
    qkv_p = qkv.reshape(NODES // K, K, 3 * C)
    keep_p = keep.reshape(NODES // K, K)
    attn = lax.map(lambda a: patch_forward(a[0], a[1], HEADS), (qkv_p, keep_p)).reshape(NODES, C)
    y_val = (input_rows.astype(jnp.float32) + jnp.dot(attn, w_out, preferred_element_type=jnp.float32)).astype(jnp.bfloat16)
    grad_wout = jnp.dot(attn.T, gt, preferred_element_type=jnp.float32) * inverse_root
    d_attn = jnp.dot(gt, w_out.T, preferred_element_type=jnp.float32).astype(jnp.bfloat16)
    d_attn_p = d_attn.reshape(NODES // K, K, C)
    d_qkv = lax.map(lambda a: patch_backward(a[0], a[1], a[2], HEADS), (qkv_p, keep_p, d_attn_p)).reshape(NODES, 3 * C)
    grad_wqkv = jnp.dot(hidden_state.T, d_qkv, preferred_element_type=jnp.float32) * inverse_root
    hidden_gradient = jnp.dot(d_qkv, w_qkv.T, preferred_element_type=jnp.float32)
    gamma_gradient = lax.optimization_barrier(jnp.sum(hidden_gradient * normalized_input, 0)) * inverse_root
    scaled_output = hidden_gradient * gamma.astype(jnp.float32)
    norm_gradient = reciprocal_deviation * (scaled_output - lax.optimization_barrier(jnp.mean(scaled_output, -1, keepdims=True)) - normalized_input * lax.optimization_barrier(jnp.mean(scaled_output * normalized_input, -1, keepdims=True)))
    d_x = (gt.astype(jnp.float32) + norm_gradient).astype(jnp.bfloat16)
    return (reorder(y_val, count, block), reorder(d_x, count, block), grad_wqkv, grad_wout, gamma_gradient)
```

```python
import functools

import jax
import jax.numpy as jnp
from jax import lax
from jax.experimental import pallas as pl
from jax.experimental.pallas import tpu as pltpu
from jax.sharding import PartitionSpec as P

HEADS = 16
K = 1024
QB = 256
MESH = pl.DeviceIdType.MESH
BF = jnp.bfloat16
F32 = jnp.float32
LOG2E = 1.4426950408889634
LIMIT = 56 * 1024 * 1024


def nn(a, b):
    return jnp.dot(a, b, preferred_element_type=F32)


def nt(a, b):
    return lax.dot_general(a, b, (((1,), (1,)), ((), ())), preferred_element_type=F32)


def place(sizes):
    nx, ny = sizes
    n = nx * ny
    me = lax.axis_index("gx") * ny + lax.axis_index("gy")
    return n, ny, me


def enter(sizes):
    n, ny, me = place(sizes)
    barrier = pltpu.get_barrier_semaphore()

    def body(i, c):
        t = lax.rem(me + i, n)
        pl.semaphore_signal(barrier, inc=1, device_id=(t // ny, lax.rem(t, ny)), device_id_type=MESH)
        return c

    lax.fori_loop(1, n, body, 0)
    pl.semaphore_wait(barrier, n - 1)


def exchange(sizes, src, dst, send, recv, one=False):
    n, ny, me = place(sizes)

    def copy(i):
        t = lax.rem(me + i, n)
        return t, pltpu.make_async_remote_copy(
            src_ref=src(t), dst_ref=dst(me), send_sem=send.at[t], recv_sem=recv.at[me],
            device_id=(t // ny, lax.rem(t, ny)), device_id_type=MESH)

    def start(i, c):
        copy(i)[1].start()
        return c

    lax.fori_loop(1, n, start, 0)


def finish(sizes, src, dst, send, recv):
    n, ny, me = place(sizes)

    def wait(i, c):
        t = lax.rem(me + i, n)
        s = lax.rem(me + n - i, n)
        pltpu.make_async_remote_copy(
            src_ref=src(t), dst_ref=dst(s), send_sem=send.at[t], recv_sem=recv.at[s],
            device_id=(t // ny, lax.rem(t, ny)), device_id_type=MESH).wait()
        return c

    lax.fori_loop(1, n, wait, 0)


def rows_of(ref, block):
    return lambda t: ref.at[pl.ds(pl.multiple_of(t * block, block), block), :]


def tile_of(ref):
    return lambda t: ref.at[t]


def inward_kernel(sizes, f_ref, c_ref, v_ref, fo_ref, co_ref, vo_ref, send, recv):
    n, ny, me = place(sizes)
    block = f_ref.shape[0] // n
    pairs = [
        (rows_of(f_ref, block), rows_of(fo_ref, block)),
        (tile_of(v_ref), tile_of(vo_ref)),
        (rows_of(c_ref, block), rows_of(co_ref, block)),
    ]
    enter(sizes)
    for k, (s, d) in enumerate(pairs):
        exchange(sizes, s, d, send.at[k], recv.at[k])
    own = pl.ds(pl.multiple_of(me * block, block), block)
    fo_ref[own, :] = f_ref[own, :]
    co_ref[own, :] = c_ref[own, :]
    vo_ref[me] = v_ref[me]
    for k, (s, d) in enumerate(pairs):
        finish(sizes, s, d, send.at[k], recv.at[k])


def outward_kernel(sizes, root, y_ref, x_ref, g_ref, yo_ref, xo_ref, gw_ref, gwo_ref, gg_ref,
                   got, mine, parts, send, recv):
    n, ny, me = place(sizes)
    block = y_ref.shape[0] // n
    width = parts.shape[2]
    pairs = [
        (tile_of(g_ref), tile_of(got)),
        (rows_of(y_ref, block), rows_of(yo_ref, block)),
        (rows_of(x_ref, block), rows_of(xo_ref, block)),
        (lambda t: mine, tile_of(parts)),
    ]
    enter(sizes)
    for k in range(3):
        s, d = pairs[k]
        exchange(sizes, s, d, send.at[k], recv.at[k])
    own = pl.ds(pl.multiple_of(me * block, block), block)
    yo_ref[own, :] = y_ref[own, :]
    xo_ref[own, :] = x_ref[own, :]
    got[me] = g_ref[me]
    finish(sizes, *pairs[0], send.at[0], recv.at[0])
    total = jnp.sum(got[...].astype(F32), 0) * root
    mine[...] = total[:, :width].astype(BF)
    exchange(sizes, *pairs[3], send.at[3], recv.at[3])
    extra = total[:, width:]
    gg_ref[:, 0:128] = extra[0:1] + extra[2:3]
    gg_ref[:, 128:256] = extra[1:2] + extra[3:4]
    parts[me] = mine[...]
    finish(sizes, *pairs[3], send.at[3], recv.at[3])
    across = 1024 // width
    for t in range(n):
        r, c = 16 * (t // across), width * (t % across)
        left = max(0, min(width, 768 - c))
        if left:
            gw_ref[r : r + 16, c : c + left] = parts[t, :, :left].astype(F32)
        if left < width:
            c0 = c + left - 768
            gwo_ref[r : r + 16, c0 : c0 + width - left] = parts[t, :, left:].astype(F32)
    for k in (1, 2):
        finish(sizes, *pairs[k], send.at[k], recv.at[k])


def split3(a):
    a1 = a.astype(BF)
    rest = a - a1.astype(F32)
    a2 = rest.astype(BF)
    a3 = (rest - a2.astype(F32)).astype(BF)
    return a1, a2, a3


def patch_kernel(n, x_ref, v_ref, g_ref, gamma_ref, wqkv_ref, wout_ref,
                 y_ref, dx_ref, gout_ref,
                 qkvt, dot_, attnt, dqkvt, hs, mask, acc, gacc, dk_acc, dv_acc):
    patch = pl.program_id(0)
    width = wout_ref.shape[0]
    x = x_ref[...].astype(F32)
    cent = x - jnp.mean(x, -1, keepdims=True)
    rstd = lax.rsqrt(jnp.mean(cent * cent, -1, keepdims=True) + 1e-05)
    gamma = gamma_ref[...]
    hs[...] = (cent * rstd * gamma).astype(BF)
    qkvt[...] = nt(wqkv_ref[...].T, hs[...]).astype(BF)
    dot_[...] = nt(wout_ref[...], g_ref[...]).astype(BF)
    first = lax.broadcasted_iota(jnp.int32, (16, 128), 0)
    for i in range(K // 128):
        per = v_ref.shape[0] // (K // 128)
        row = v_ref[per * i].astype(F32)
        for j in range(1, per):
            row = row + v_ref[per * i + j].astype(F32)
        bias = jnp.where(row > 0.5, 0.0, -1e30)
        mask[:, i * 128 : (i + 1) * 128] = jnp.where(first == 0, bias, 0.0).astype(BF)

    def head(h, carry):
        base = pl.multiple_of(h * 16, 16)
        qt = qkvt[pl.ds(base, 16), :]
        kt = qkvt[pl.ds(pl.multiple_of(width + base, 16), 16), :]
        vt = qkvt[pl.ds(pl.multiple_of(2 * width + base, 16), 16), :]
        q1, q2, q3 = split3(qt.astype(F32) * (0.25 * LOG2E))
        ones = jnp.ones((16, K), BF)
        qa = jnp.concatenate([q1, q2, q3, ones], 0)
        ka = jnp.concatenate([kt, kt, kt, mask[...]], 0).T
        va = jnp.concatenate([vt, ones], 0)
        v2 = jnp.concatenate([vt, vt, ones], 0).T
        rows = lax.broadcasted_iota(jnp.int32, (16, QB), 0)
        for b in range(K // QB):
            cols = slice(b * QB, (b + 1) * QB)
            st = nn(ka, qa[:, cols])
            top = jnp.max(st, 0, keepdims=True)
            e32 = jnp.exp2(st - top)
            e = e32.astype(BF)
            ot = nn(va, e)
            r = 1.0 / ot[16:17]
            o = ot[:16] * r
            attnt[pl.ds(base, 16), cols] = o.astype(BF)
            do = dot_[pl.ds(base, 16), cols].astype(F32)
            delta = jnp.sum(do * o, 0, keepdims=True)
            rs = r * 0.25
            a = do * rs
            a1 = a.astype(BF)
            a2 = (a - a1.astype(F32)).astype(BF)
            b1, b2, b3 = split3(-delta * rs)
            low = jnp.where(
                rows == 0, b1.astype(F32),
                jnp.where(rows == 1, b2.astype(F32), jnp.where(rows == 2, b3.astype(F32), 0.0)),
            ).astype(BF)
            both = jnp.concatenate([a1, a2], 0)
            dt = nn(v2, jnp.concatenate([both, low], 0))
            ds = (e32 * dt).astype(BF)
            dqkvt[pl.ds(base, 16), cols] = nn(kt, ds).astype(BF)
            dk = nt(qt[:, cols], ds)
            dv = nt(both, e)
            if b == 0:
                dk_acc[...] = dk
                dv_acc[...] = dv
            else:
                dk_acc[...] += dk
                dv_acc[...] += dv
        dqkvt[pl.ds(pl.multiple_of(width + base, 16), 16), :] = dk_acc[...].astype(BF)
        dqkvt[pl.ds(pl.multiple_of(2 * width + base, 16), 16), :] = (
            4.0 * (dv_acc[:16] + dv_acc[16:])
        ).astype(BF)
        return carry

    lax.fori_loop(0, HEADS, head, 0)

    x = x_ref[...].astype(F32)
    attn = attnt[...].T
    y_ref[...] = (x + nn(attn, wout_ref[...])).astype(BF)
    local_wout = nn(attnt[...], g_ref[...])
    local_wqkv = nn(dqkvt[...], hs[...]).T
    dh = nt(dqkvt[...].T, wqkv_ref[...])
    cent = x - jnp.mean(x, -1, keepdims=True)
    rstd = lax.rsqrt(jnp.mean(cent * cent, -1, keepdims=True) + 1e-05)
    xhat = cent * rstd
    local_gamma = jnp.sum(dh * xhat, 0, keepdims=True)
    g = dh * gamma
    dx = rstd * (g - jnp.mean(g, -1, keepdims=True) - xhat * jnp.mean(g * xhat, -1, keepdims=True))
    dx_ref[...] = (g_ref[...].astype(F32) + dx).astype(BF)

    @pl.when(patch == 0)
    def _():
        acc[:, :768] = local_wqkv
        acc[:, 768:] = local_wout
        gacc[...] = local_gamma

    @pl.when(patch > 0)
    def _():
        acc[:, :768] += local_wqkv
        acc[:, 768:] += local_wout
        gacc[...] += local_gamma

    @pl.when(patch == pl.num_programs(0) - 1)
    def _():
        w = gout_ref.shape[2] - 128
        across = 1024 // w
        total = gacc[...]
        hi = total.astype(BF).astype(F32)
        lo = total - hi
        rows = lax.broadcasted_iota(jnp.int32, (16, 128), 0)
        extra = jnp.where(
            rows == 0, hi[:, :128],
            jnp.where(rows == 1, hi[:, 128:],
                      jnp.where(rows == 2, lo[:, :128], jnp.where(rows == 3, lo[:, 128:], 0.0))),
        ).astype(BF)
        for t in range(n):
            r, c = 16 * (t // across), w * (t % across)
            gout_ref[t, :, :w] = acc[r : r + 16, c : c + w].astype(BF)
            gout_ref[t, :, w:] = extra


def shards(sizes, features, valid, cotangent, gamma, w_qkv, w_out):
    n = sizes[0] * sizes[1]
    rows, width = features.shape
    patches = rows // K
    block = rows // n
    root = float(rows * n) ** (-0.5)
    me = lax.axis_index("gx") * sizes[1] + lax.axis_index("gy")
    lane = jnp.arange(128, dtype=jnp.int32) // block
    spread = jnp.tile(valid.reshape(n, block), (1, 128 // block))
    spread = jnp.where(lane[None, :] == lax.rem(me, 128 // block), spread, 0).astype(BF)
    spread = jnp.broadcast_to(spread[:, None, :], (n, 16, 128))

    vmem = pl.BlockSpec(memory_space=pltpu.VMEM)
    node = jax.ShapeDtypeStruct((rows, width), BF)
    xt, gt, vt = pl.pallas_call(
        functools.partial(inward_kernel, sizes),
        out_shape=(node, node, jax.ShapeDtypeStruct((n, 16, 128), BF)),
        in_specs=[vmem] * 3,
        out_specs=(vmem,) * 3,
        scratch_shapes=[pltpu.SemaphoreType.DMA((3, n)), pltpu.SemaphoreType.DMA((3, n))],
        compiler_params=pltpu.CompilerParams(collective_id=0, has_side_effects=True, vmem_limit_bytes=LIMIT),
        name="inward",
    )(features, cotangent, spread)

    tile = 16384 // n
    row_spec = pl.BlockSpec((K, width), lambda i: (i, 0))

    def whole(shape):
        return pl.BlockSpec(shape, lambda i: (0,) * len(shape))

    y, dx, grads = pl.pallas_call(
        functools.partial(patch_kernel, n),
        grid=(patches,),
        out_shape=(node, node, jax.ShapeDtypeStruct((n, 16, tile + 128), BF)),
        in_specs=[
            row_spec,
            pl.BlockSpec((K // block, 16, 128), lambda i: (i, 0, 0)),
            row_spec,
            whole((1, width)),
            whole((width, 3 * width)),
            whole((width, width)),
        ],
        out_specs=(row_spec, row_spec, whole((n, 16, tile + 128))),
        scratch_shapes=[
            pltpu.VMEM((3 * width, K), BF),
            pltpu.VMEM((width, K), BF),
            pltpu.VMEM((width, K), BF),
            pltpu.VMEM((3 * width, K), BF),
            pltpu.VMEM((K, width), BF),
            pltpu.VMEM((16, K), BF),
            pltpu.VMEM((width, 4 * width), F32),
            pltpu.VMEM((1, width), F32),
            pltpu.VMEM((16, K), F32),
            pltpu.VMEM((32, K), F32),
        ],
        compiler_params=pltpu.CompilerParams(
            dimension_semantics=("arbitrary",), vmem_limit_bytes=LIMIT),
        name="patch",
    )(xt, vt, gt, gamma.reshape(1, width), w_qkv, w_out)

    y_plain, dx_plain, gw, gwo, gg = pl.pallas_call(
        functools.partial(outward_kernel, sizes, root),
        out_shape=(
            node, node,
            jax.ShapeDtypeStruct((width, 3 * width), F32),
            jax.ShapeDtypeStruct((width, width), F32),
            jax.ShapeDtypeStruct((1, width), F32),
        ),
        in_specs=[vmem] * 3,
        out_specs=(vmem,) * 5,
        scratch_shapes=[
            pltpu.VMEM((n, 16, tile + 128), BF),
            pltpu.VMEM((16, tile), BF),
            pltpu.VMEM((n, 16, tile), BF),
            pltpu.SemaphoreType.DMA((4, n)),
            pltpu.SemaphoreType.DMA((4, n)),
        ],
        compiler_params=pltpu.CompilerParams(collective_id=1, has_side_effects=True, vmem_limit_bytes=LIMIT),
        name="outward",
    )(y, dx, grads)
    return y_plain, dx_plain, gw, gwo, gg.reshape(width)


def solution(mesh):
    sizes = (mesh.shape["gx"], mesh.shape["gy"])
    both = P(("gx", "gy"), None)
    return jax.shard_map(
        functools.partial(shards, sizes),
        mesh=mesh,
        in_specs=(both, P(("gx", "gy")), both, P(), P(), P()),
        out_specs=(both, both, P(), P(), P()),
        check_vma=False,
    )
```

```python
import functools

import jax
import jax.numpy as jnp
from jax import lax
from jax.experimental import pallas as pl
from jax.experimental.pallas import tpu as pltpu
from jax.sharding import PartitionSpec as P

HEADS = 16
K = 1024
QB = 1024
MESH = pl.DeviceIdType.MESH
BF = jnp.bfloat16
F32 = jnp.float32
LOG2E = 1.4426950408889634
LIMIT = 56 * 1024 * 1024


def nn(a, b):
    return jnp.dot(a, b, preferred_element_type=F32)


def nt(a, b):
    return lax.dot_general(a, b, (((1,), (1,)), ((), ())), preferred_element_type=F32)


def place(sizes):
    nx, ny = sizes
    n = nx * ny
    me = lax.axis_index("gx") * ny + lax.axis_index("gy")
    return n, ny, me


def enter(sizes):
    n, ny, me = place(sizes)
    barrier = pltpu.get_barrier_semaphore()

    def body(i, c):
        t = lax.rem(me + i, n)
        pl.semaphore_signal(barrier, inc=1, device_id=(t // ny, lax.rem(t, ny)), device_id_type=MESH)
        return c

    lax.fori_loop(1, n, body, 0)
    pl.semaphore_wait(barrier, n - 1)


def exchange(sizes, src, dst, send, recv, one=False):
    n, ny, me = place(sizes)

    def copy(i):
        t = lax.rem(me + i, n)
        return t, pltpu.make_async_remote_copy(
            src_ref=src(t), dst_ref=dst(me), send_sem=send.at[t], recv_sem=recv.at[me],
            device_id=(t // ny, lax.rem(t, ny)), device_id_type=MESH)

    def start(i, c):
        copy(i)[1].start()
        return c

    lax.fori_loop(1, n, start, 0)


def finish(sizes, src, dst, send, recv):
    n, ny, me = place(sizes)

    def wait(i, c):
        t = lax.rem(me + i, n)
        s = lax.rem(me + n - i, n)
        pltpu.make_async_remote_copy(
            src_ref=src(t), dst_ref=dst(s), send_sem=send.at[t], recv_sem=recv.at[s],
            device_id=(t // ny, lax.rem(t, ny)), device_id_type=MESH).wait()
        return c

    lax.fori_loop(1, n, wait, 0)


def rows_of(ref, block):
    return lambda t: ref.at[pl.ds(pl.multiple_of(t * block, block), block), :]


def tile_of(ref):
    return lambda t: ref.at[t]


def inward_kernel(sizes, f_ref, c_ref, v_ref, fo_ref, co_ref, vo_ref, send, recv):
    n, ny, me = place(sizes)
    block = f_ref.shape[0] // n
    pairs = [
        (rows_of(f_ref, block), rows_of(fo_ref, block)),
        (tile_of(v_ref), tile_of(vo_ref)),
        (rows_of(c_ref, block), rows_of(co_ref, block)),
    ]
    enter(sizes)
    for k, (s, d) in enumerate(pairs):
        exchange(sizes, s, d, send.at[k], recv.at[k])
    own = pl.ds(pl.multiple_of(me * block, block), block)
    fo_ref[own, :] = f_ref[own, :]
    co_ref[own, :] = c_ref[own, :]
    vo_ref[me] = v_ref[me]
    for k, (s, d) in enumerate(pairs):
        finish(sizes, s, d, send.at[k], recv.at[k])


def parted(left, right, width):
    rows = lax.broadcasted_iota(jnp.int32, (16, 128), 0)
    hi_l, hi_r = left.astype(BF).astype(F32), right.astype(BF).astype(F32)
    block = jnp.where(
        rows == 0, hi_l,
        jnp.where(rows == 1, hi_r,
                  jnp.where(rows == 2, left - hi_l, jnp.where(rows == 3, right - hi_r, 0.0))),
    )
    if width > 128:
        block = jnp.concatenate([block, jnp.zeros((16, width - 128), F32)], 1)
    return block.astype(BF)


def outward_kernel(sizes, root, y_ref, x_ref, g_ref, yo_ref, xo_ref, gw_ref, gwo_ref, gg_ref,
                   got, half, seen, fine, parts, send, recv, s1, r1, s2, r2, s3, r3):
    nx, ny = sizes
    n, _, me = place(sizes)
    mx, my = lax.axis_index("gx"), lax.axis_index("gy")
    block = x_ref.shape[0] // n
    width = parts.shape[2]
    body = 16 * ny

    def across(size, mine, src, dst, send, recv, along_x):
        for i in range(1, size):
            t = lax.rem(mine + i, size)
            pltpu.make_async_remote_copy(
                src_ref=src(t), dst_ref=dst(mine), send_sem=send.at[t], recv_sem=recv.at[mine],
                device_id=(t, my) if along_x else (mx, t), device_id_type=MESH).start()

    def settle(size, mine, src, dst, send, recv, along_x):
        for i in range(1, size):
            t = lax.rem(mine + i, size)
            s = lax.rem(mine + size - i, size)
            pltpu.make_async_remote_copy(
                src_ref=src(t), dst_ref=dst(s), send_sem=send.at[t], recv_sem=recv.at[s],
                device_id=(t, my) if along_x else (mx, t), device_id_type=MESH).wait()

    first = (nx, mx, tile_of(g_ref), tile_of(got), s1, r1, True)
    second = (ny, my, lambda t: half, tile_of(seen), s2, r2, False)
    third = (nx, mx, lambda t: fine, tile_of(parts), s3, r3, True)
    nodes = [(rows_of(y_ref, block), rows_of(yo_ref, block)), (rows_of(x_ref, block), rows_of(xo_ref, block))]
    enter(sizes)
    across(*first)
    for k in range(2):
        exchange(sizes, *nodes[k], send.at[k], recv.at[k])
    own = pl.ds(pl.multiple_of(me * block, block), block)
    yo_ref[own, :] = y_ref[own, :]
    xo_ref[own, :] = x_ref[own, :]
    got[mx] = g_ref[mx]
    settle(*first)
    total = jnp.sum(got[...].astype(F32), 0)
    extra = total[body:, :128]
    half[:body, :] = total[:body].astype(BF)
    half[body:, :] = parted(extra[0:1] + extra[2:3], extra[1:2] + extra[3:4], width)
    across(*second)
    seen[my] = half[...]
    settle(*second)
    total = jnp.sum(seen[...].astype(F32), 0) * root
    fine[...] = total[:body].astype(BF)
    across(*third)
    extra = total[body:, :128]
    gg_ref[:, 0:128] = extra[0:1] + extra[2:3]
    gg_ref[:, 128:256] = extra[1:2] + extra[3:4]
    parts[mx] = fine[...]
    settle(*third)
    side = 1024 // width
    for t in range(n):
        r, c = 16 * (t // side), width * (t % side)
        r0 = 16 * (t % ny)
        left = max(0, min(width, 768 - c))
        if left:
            gw_ref[r : r + 16, c : c + left] = parts[t // ny, r0 : r0 + 16, :left].astype(F32)
        if left < width:
            c0 = c + left - 768
            gwo_ref[r : r + 16, c0 : c0 + width - left] = parts[t // ny, r0 : r0 + 16, left:].astype(F32)
    for k in range(2):
        finish(sizes, *nodes[k], send.at[k], recv.at[k])


def split3(a):
    a1 = a.astype(BF)
    rest = a - a1.astype(F32)
    a2 = rest.astype(BF)
    a3 = (rest - a2.astype(F32)).astype(BF)
    return a1, a2, a3


def patch_kernel(sizes, x_ref, v_ref, g_ref, gamma_ref, wqkv_ref, wout_ref,
                 y_ref, dx_ref, gout_ref,
                 qkvt, dot_, attnt, dqkvt, hs, mask, acc, gacc, dk_acc, dv_acc):
    patch = pl.program_id(0)
    width = wout_ref.shape[0]
    x = x_ref[...].astype(F32)
    cent = x - jnp.mean(x, -1, keepdims=True)
    rstd = lax.rsqrt(jnp.mean(cent * cent, -1, keepdims=True) + 1e-05)
    gamma = gamma_ref[...]
    hs[...] = (cent * rstd * gamma).astype(BF)
    qkvt[...] = nt(wqkv_ref[...].T, hs[...]).astype(BF)
    dot_[...] = nt(wout_ref[...], g_ref[...]).astype(BF)
    first = lax.broadcasted_iota(jnp.int32, (16, 128), 0)
    for i in range(K // 128):
        per = v_ref.shape[0] // (K // 128)
        row = v_ref[per * i]
        for j in range(1, per):
            row = row + v_ref[per * i + j]
        bias = jnp.where(row > 0.5, 0.0, -1e30)
        mask[:, i * 128 : (i + 1) * 128] = jnp.where(first == 0, bias, 0.0).astype(BF)

    def head(h, carry):
        base = pl.multiple_of(h * 16, 16)
        qt = qkvt[pl.ds(base, 16), :]
        kt = qkvt[pl.ds(pl.multiple_of(width + base, 16), 16), :]
        vt = qkvt[pl.ds(pl.multiple_of(2 * width + base, 16), 16), :]
        q1, q2, q3 = split3(qt.astype(F32) * (0.25 * LOG2E))
        ones = jnp.ones((16, K), BF)
        qa = jnp.concatenate([q1, q2, q3, ones], 0)
        ka = jnp.concatenate([kt, kt, kt, mask[...]], 0).T
        va = jnp.concatenate([vt, ones], 0)
        v2 = jnp.concatenate([vt, vt, ones], 0).T
        rows = lax.broadcasted_iota(jnp.int32, (16, QB), 0)
        for b in range(K // QB):
            cols = slice(b * QB, (b + 1) * QB)
            st = nn(ka, qa[:, cols])
            top = jnp.max(st, 0, keepdims=True)
            e32 = jnp.exp2(st - top)
            e = e32.astype(BF)
            ot = nn(va, e)
            r = 1.0 / ot[16:17]
            o = ot[:16] * r
            attnt[pl.ds(base, 16), cols] = o.astype(BF)
            do = dot_[pl.ds(base, 16), cols].astype(F32)
            delta = jnp.sum(do * o, 0, keepdims=True)
            rs = r * 0.25
            a = do * rs
            a1 = a.astype(BF)
            a2 = (a - a1.astype(F32)).astype(BF)
            b1, b2, b3 = split3(-delta * rs)
            low = jnp.where(
                rows == 0, b1.astype(F32),
                jnp.where(rows == 1, b2.astype(F32), jnp.where(rows == 2, b3.astype(F32), 0.0)),
            ).astype(BF)
            both = jnp.concatenate([a1, a2], 0)
            dt = nn(v2, jnp.concatenate([both, low], 0))
            ds = (e32 * dt).astype(BF)
            dqkvt[pl.ds(base, 16), cols] = nn(kt, ds).astype(BF)
            dk = nt(qt[:, cols], ds)
            dv = nt(both, e)
            if b == 0:
                dk_acc[...] = dk
                dv_acc[...] = dv
            else:
                dk_acc[...] += dk
                dv_acc[...] += dv
        dqkvt[pl.ds(pl.multiple_of(width + base, 16), 16), :] = dk_acc[...].astype(BF)
        dqkvt[pl.ds(pl.multiple_of(2 * width + base, 16), 16), :] = (
            4.0 * (dv_acc[:16] + dv_acc[16:])
        ).astype(BF)
        return carry

    lax.fori_loop(0, HEADS, head, 0)

    x = x_ref[...].astype(F32)
    attn = attnt[...].T
    y_ref[...] = (x + nn(attn, wout_ref[...])).astype(BF)
    local_wout = nn(attnt[...], g_ref[...])
    local_wqkv = nn(dqkvt[...], hs[...]).T
    dh = nt(dqkvt[...].T, wqkv_ref[...])
    cent = x - jnp.mean(x, -1, keepdims=True)
    rstd = lax.rsqrt(jnp.mean(cent * cent, -1, keepdims=True) + 1e-05)
    xhat = cent * rstd
    local_gamma = jnp.sum(dh * xhat, 0, keepdims=True)
    g = dh * gamma
    dx = rstd * (g - jnp.mean(g, -1, keepdims=True) - xhat * jnp.mean(g * xhat, -1, keepdims=True))
    dx_ref[...] = (g_ref[...].astype(F32) + dx).astype(BF)

    @pl.when(patch == 0)
    def _():
        acc[:, :768] = local_wqkv
        acc[:, 768:] = local_wout
        gacc[...] = local_gamma

    @pl.when(patch > 0)
    def _():
        acc[:, :768] += local_wqkv
        acc[:, 768:] += local_wout
        gacc[...] += local_gamma

    @pl.when(patch == pl.num_programs(0) - 1)
    def _():
        nx, ny = sizes
        w = gout_ref.shape[2]
        across = 1024 // w
        total = gacc[...]
        extra = parted(total[:, :128], total[:, 128:], w)
        for t in range(nx * ny):
            r, c = 16 * (t // across), w * (t % across)
            r0 = 16 * (t % ny)
            gout_ref[t // ny, r0 : r0 + 16, :] = acc[r : r + 16, c : c + w].astype(BF)
        for t in range(nx):
            gout_ref[t, 16 * ny :, :] = extra


def shards(sizes, features, valid, cotangent, gamma, w_qkv, w_out):
    n = sizes[0] * sizes[1]
    rows, width = features.shape
    patches = rows // K
    block = rows // n
    root = float(rows * n) ** (-0.5)
    me = lax.axis_index("gx") * sizes[1] + lax.axis_index("gy")
    lane = jnp.arange(128, dtype=jnp.int32) // block
    spread = jnp.tile(valid.reshape(n, block), (1, 128 // block))
    spread = jnp.where(lane[None, :] == lax.rem(me, 128 // block), spread, 0).astype(F32)[:, None, :]

    vmem = pl.BlockSpec(memory_space=pltpu.VMEM)
    node = jax.ShapeDtypeStruct((rows, width), BF)
    xt, gt, vt = pl.pallas_call(
        functools.partial(inward_kernel, sizes),
        out_shape=(node, node, jax.ShapeDtypeStruct((n, 1, 128), F32)),
        in_specs=[vmem] * 3,
        out_specs=(vmem,) * 3,
        scratch_shapes=[pltpu.SemaphoreType.DMA((3, n)), pltpu.SemaphoreType.DMA((3, n))],
        compiler_params=pltpu.CompilerParams(collective_id=0, has_side_effects=True, vmem_limit_bytes=LIMIT),
        name="inward",
    )(features, cotangent, spread)

    tile = 16384 // n
    nx, ny = sizes
    row_spec = pl.BlockSpec((K, width), lambda i: (i, 0))

    def whole(shape):
        return pl.BlockSpec(shape, lambda i: (0,) * len(shape))

    y, dx, grads = pl.pallas_call(
        functools.partial(patch_kernel, sizes),
        grid=(patches,),
        out_shape=(node, node, jax.ShapeDtypeStruct((nx, 16 * ny + 16, tile), BF)),
        in_specs=[
            row_spec,
            pl.BlockSpec((K // block, 1, 128), lambda i: (i, 0, 0)),
            row_spec,
            whole((1, width)),
            whole((width, 3 * width)),
            whole((width, width)),
        ],
        out_specs=(row_spec, row_spec, whole((nx, 16 * ny + 16, tile))),
        scratch_shapes=[
            pltpu.VMEM((3 * width, K), BF),
            pltpu.VMEM((width, K), BF),
            pltpu.VMEM((width, K), BF),
            pltpu.VMEM((3 * width, K), BF),
            pltpu.VMEM((K, width), BF),
            pltpu.VMEM((16, K), BF),
            pltpu.VMEM((width, 4 * width), F32),
            pltpu.VMEM((1, width), F32),
            pltpu.VMEM((16, K), F32),
            pltpu.VMEM((32, K), F32),
        ],
        compiler_params=pltpu.CompilerParams(
            dimension_semantics=("arbitrary",), vmem_limit_bytes=LIMIT),
        name="patch",
    )(xt, vt, gt, gamma.reshape(1, width), w_qkv, w_out)

    y_plain, dx_plain, gw, gwo, gg = pl.pallas_call(
        functools.partial(outward_kernel, sizes, root),
        out_shape=(
            node, node,
            jax.ShapeDtypeStruct((width, 3 * width), F32),
            jax.ShapeDtypeStruct((width, width), F32),
            jax.ShapeDtypeStruct((1, width), F32),
        ),
        in_specs=[vmem] * 3,
        out_specs=(vmem,) * 5,
        scratch_shapes=[
            pltpu.VMEM((nx, 16 * ny + 16, tile), BF),
            pltpu.VMEM((16 * ny + 16, tile), BF),
            pltpu.VMEM((ny, 16 * ny + 16, tile), BF),
            pltpu.VMEM((16 * ny, tile), BF),
            pltpu.VMEM((nx, 16 * ny, tile), BF),
            pltpu.SemaphoreType.DMA((2, n)),
            pltpu.SemaphoreType.DMA((2, n)),
        ] + [pltpu.SemaphoreType.DMA((size,)) for size in (nx, nx, ny, ny, nx, nx)],
        compiler_params=pltpu.CompilerParams(collective_id=1, has_side_effects=True, vmem_limit_bytes=LIMIT),
        name="outward",
    )(y, dx, grads)
    return y_plain, dx_plain, gw, gwo, gg.reshape(width)


def solution(mesh):
    sizes = (mesh.shape["gx"], mesh.shape["gy"])
    both = P(("gx", "gy"), None)
    return jax.shard_map(
        functools.partial(shards, sizes),
        mesh=mesh,
        in_specs=(both, P(("gx", "gy")), both, P(), P(), P()),
        out_specs=(both, both, P(), P(), P()),
        check_vma=False,
    )
```

```python
import functools

import jax
import jax.numpy as jnp
from jax import lax
from jax.experimental import pallas as pl
from jax.experimental.pallas import tpu as pltpu
from jax.sharding import PartitionSpec as P

HEADS = 16
K = 1024
MESH = pl.DeviceIdType.MESH
BF = jnp.bfloat16
F32 = jnp.float32
LOG2E = 1.4426950408889634
LIMIT = 56 * 1024 * 1024


def nn(a, b):
    return jnp.dot(a, b, preferred_element_type=F32)


def nt(a, b):
    return lax.dot_general(a, b, (((1,), (1,)), ((), ())), preferred_element_type=F32)


def place(sizes):
    nx, ny = sizes
    n = nx * ny
    me = lax.axis_index("gx") * ny + lax.axis_index("gy")
    return n, ny, me


def enter(sizes):
    n, ny, me = place(sizes)
    barrier = pltpu.get_barrier_semaphore()

    def body(i, c):
        t = lax.rem(me + i, n)
        pl.semaphore_signal(barrier, inc=1, device_id=(t // ny, lax.rem(t, ny)), device_id_type=MESH)
        return c

    lax.fori_loop(1, n, body, 0)
    pl.semaphore_wait(barrier, n - 1)


def exchange(sizes, src, dst, send, recv, one=False):
    n, ny, me = place(sizes)

    def copy(i):
        t = lax.rem(me + i, n)
        return t, pltpu.make_async_remote_copy(
            src_ref=src(t), dst_ref=dst(me), send_sem=send.at[t], recv_sem=recv.at[me],
            device_id=(t // ny, lax.rem(t, ny)), device_id_type=MESH)

    def start(i, c):
        copy(i)[1].start()
        return c

    lax.fori_loop(1, n, start, 0)


def finish(sizes, src, dst, send, recv):
    n, ny, me = place(sizes)

    def wait(i, c):
        t = lax.rem(me + i, n)
        s = lax.rem(me + n - i, n)
        pltpu.make_async_remote_copy(
            src_ref=src(t), dst_ref=dst(s), send_sem=send.at[t], recv_sem=recv.at[s],
            device_id=(t // ny, lax.rem(t, ny)), device_id_type=MESH).wait()
        return c

    lax.fori_loop(1, n, wait, 0)


def rows_of(ref, block):
    return lambda t: ref.at[pl.ds(pl.multiple_of(t * block, block), block), :]


def tile_of(ref):
    return lambda t: ref.at[t]


def parted(left, right, width):
    rows = lax.broadcasted_iota(jnp.int32, (16, 128), 0)
    hi_l, hi_r = left.astype(BF).astype(F32), right.astype(BF).astype(F32)
    block = jnp.where(
        rows == 0, hi_l,
        jnp.where(rows == 1, hi_r,
                  jnp.where(rows == 2, left - hi_l, jnp.where(rows == 3, right - hi_r, 0.0))),
    )
    if width > 128:
        block = jnp.concatenate([block, jnp.zeros((16, width - 128), F32)], 1)
    return block.astype(BF)


def outward_kernel(sizes, root, x_ref, g_ref, xo_ref, gw_ref, gwo_ref, gg_ref,
                   got, half, seen, fine, parts, send, recv, s1, r1, s2, r2, s3, r3):
    nx, ny = sizes
    n, _, me = place(sizes)
    mx, my = lax.axis_index("gx"), lax.axis_index("gy")
    block = x_ref.shape[0] // n
    width = parts.shape[2]
    body = 16 * ny

    def across(size, mine, src, dst, send, recv, along_x):
        for i in range(1, size):
            t = lax.rem(mine + i, size)
            pltpu.make_async_remote_copy(
                src_ref=src(t), dst_ref=dst(mine), send_sem=send.at[t], recv_sem=recv.at[mine],
                device_id=(t, my) if along_x else (mx, t), device_id_type=MESH).start()

    def settle(size, mine, src, dst, send, recv, along_x):
        for i in range(1, size):
            t = lax.rem(mine + i, size)
            s = lax.rem(mine + size - i, size)
            pltpu.make_async_remote_copy(
                src_ref=src(t), dst_ref=dst(s), send_sem=send.at[t], recv_sem=recv.at[s],
                device_id=(t, my) if along_x else (mx, t), device_id_type=MESH).wait()

    first = (nx, mx, tile_of(g_ref), tile_of(got), s1, r1, True)
    second = (ny, my, lambda t: half, tile_of(seen), s2, r2, False)
    third = (nx, mx, lambda t: fine, tile_of(parts), s3, r3, True)
    nodes = (rows_of(x_ref, block), rows_of(xo_ref, block))
    enter(sizes)
    across(*first)
    exchange(sizes, *nodes, send, recv)
    own = pl.ds(pl.multiple_of(me * block, block), block)
    xo_ref[own, :] = x_ref[own, :]
    got[mx] = g_ref[mx]
    settle(*first)
    total = jnp.sum(got[...].astype(F32), 0)
    extra = total[body:, :128]
    half[:body, :] = total[:body].astype(BF)
    half[body:, :] = parted(extra[0:1] + extra[2:3], extra[1:2] + extra[3:4], width)
    across(*second)
    seen[my] = half[...]
    settle(*second)
    total = jnp.sum(seen[...].astype(F32), 0) * root
    fine[...] = total[:body].astype(BF)
    across(*third)
    extra = total[body:, :128]
    gg_ref[:, 0:128] = extra[0:1] + extra[2:3]
    gg_ref[:, 128:256] = extra[1:2] + extra[3:4]
    parts[mx] = fine[...]
    settle(*third)
    side = 1024 // width
    for t in range(n):
        r, c = 16 * (t // side), width * (t % side)
        r0 = 16 * (t % ny)
        left = max(0, min(width, 768 - c))
        if left:
            gw_ref[r : r + 16, c : c + left] = parts[t // ny, r0 : r0 + 16, :left].astype(F32)
        if left < width:
            c0 = c + left - 768
            gwo_ref[r : r + 16, c0 : c0 + width - left] = parts[t // ny, r0 : r0 + 16, left:].astype(F32)
    finish(sizes, *nodes, send, recv)


def split3(a):
    a1 = a.astype(BF)
    rest = a - a1.astype(F32)
    a2 = rest.astype(BF)
    a3 = (rest - a2.astype(F32)).astype(BF)
    return a1, a2, a3


def norm(x_ref):
    x = x_ref[...].astype(F32)
    cent = x - jnp.mean(x, -1, keepdims=True)
    rstd = lax.rsqrt(jnp.mean(cent * cent, -1, keepdims=True) + 1e-05)
    return cent * rstd, rstd


def patch_kernel(sizes, f_ref, v_ref, c_ref, gamma_ref, wqkv_ref, wout_ref,
                 yo_ref, dx_ref, gout_ref,
                 x_ref, vo_ref, g_ref, y_ref, e_ref, ot_ref, inv_ref,
                 qkvt, dot_, attnt, dqkvt, hs, mask, send, recv):
    n, ny, me = place(sizes)
    nx = sizes[0]
    width = wout_ref.shape[0]
    block = f_ref.shape[0] // n
    own = pl.ds(pl.multiple_of(me * block, block), block)
    features = (rows_of(f_ref, block), rows_of(x_ref, block), send.at[0], recv.at[0])
    occupied = (tile_of(v_ref), tile_of(vo_ref), send.at[1], recv.at[1])
    cotangent = (rows_of(c_ref, block), rows_of(g_ref, block), send.at[2], recv.at[2])
    result = (rows_of(y_ref, block), rows_of(yo_ref, block), send.at[3], recv.at[3])
    enter(sizes)
    exchange(sizes, *features)
    exchange(sizes, *occupied)
    x_ref[own, :] = f_ref[own, :]
    vo_ref[me] = v_ref[me]
    g_ref[own, :] = c_ref[own, :]
    finish(sizes, *features)
    finish(sizes, *occupied)
    exchange(sizes, *cotangent)

    gamma = gamma_ref[...]
    hs[...] = (norm(x_ref)[0] * gamma).astype(BF)
    qkvt[...] = nt(wqkv_ref[...].T, hs[...]).astype(BF)
    first = lax.broadcasted_iota(jnp.int32, (16, 128), 0)
    per = n // (K // 128)
    for i in range(K // 128):
        row = vo_ref[per * i]
        for j in range(1, per):
            row = row + vo_ref[per * i + j]
        bias = jnp.where(row > 0.5, 0.0, -1e30)
        mask[:, i * 128 : (i + 1) * 128] = jnp.where(first == 0, bias, 0.0).astype(BF)

    def parts_of(h):
        base = pl.multiple_of(h * 16, 16)
        return (pl.ds(base, 16), pl.ds(pl.multiple_of(width + base, 16), 16),
                pl.ds(pl.multiple_of(2 * width + base, 16), 16))

    def ahead(h, carry):
        at_q, at_k, at_v = parts_of(h)
        kt = qkvt[at_k, :]
        q1, q2, q3 = split3(qkvt[at_q, :].astype(F32) * (0.25 * LOG2E))
        ones = jnp.ones((16, K), BF)
        ka = jnp.concatenate([kt, kt, kt, mask[...]], 0).T
        st = nn(ka, jnp.concatenate([q1, q2, q3, ones], 0))
        e = jnp.exp2(st - jnp.max(st, 0, keepdims=True)).astype(BF)
        e_ref[h] = e
        ot = nn(jnp.concatenate([qkvt[at_v, :], ones], 0), e)
        r = 1.0 / ot[16:17]
        o = ot[:16] * r
        ot_ref[at_q, :] = o
        attnt[at_q, :] = o.astype(BF)
        inv_ref[h] = jnp.broadcast_to(r, (8, K))
        return carry

    lax.fori_loop(0, HEADS, ahead, 0)
    y_ref[...] = (x_ref[...].astype(F32) + nn(attnt[...].T, wout_ref[...])).astype(BF)
    finish(sizes, *cotangent)
    exchange(sizes, *result)
    yo_ref[own, :] = y_ref[own, :]
    dot_[...] = nt(wout_ref[...], g_ref[...]).astype(BF)

    def back(h, carry):
        at_q, at_k, at_v = parts_of(h)
        vt = qkvt[at_v, :]
        rows = lax.broadcasted_iota(jnp.int32, (16, K), 0)
        v2 = jnp.concatenate([vt, vt, jnp.ones((16, K), BF)], 0).T
        e = e_ref[h]
        do = dot_[at_q, :].astype(F32)
        delta = jnp.sum(do * ot_ref[at_q, :], 0, keepdims=True)
        rs = inv_ref[h, 0:1, :] * 0.25
        a = do * rs
        a1 = a.astype(BF)
        a2 = (a - a1.astype(F32)).astype(BF)
        b1, b2, b3 = split3(-delta * rs)
        low = jnp.where(
            rows == 0, b1.astype(F32),
            jnp.where(rows == 1, b2.astype(F32), jnp.where(rows == 2, b3.astype(F32), 0.0)),
        ).astype(BF)
        both = jnp.concatenate([a1, a2], 0)
        dt = nn(v2, jnp.concatenate([both, low], 0))
        ds = (e.astype(F32) * dt).astype(BF)
        dqkvt[at_q, :] = nn(qkvt[at_k, :], ds).astype(BF)
        dqkvt[at_k, :] = nt(qkvt[at_q, :], ds).astype(BF)
        dv = nt(both, e)
        dqkvt[at_v, :] = (4.0 * (dv[:16] + dv[16:])).astype(BF)
        return carry

    lax.fori_loop(0, HEADS, back, 0)

    local_wout = nn(attnt[...], g_ref[...])
    local_wqkv = nn(dqkvt[...], hs[...]).T
    dh = nt(dqkvt[...].T, wqkv_ref[...])
    xhat, rstd = norm(x_ref)
    total = jnp.sum(dh * xhat, 0, keepdims=True)
    g = dh * gamma
    dx = rstd * (g - jnp.mean(g, -1, keepdims=True) - xhat * jnp.mean(g * xhat, -1, keepdims=True))
    dx_ref[...] = (g_ref[...].astype(F32) + dx).astype(BF)
    w = gout_ref.shape[2]
    across = 1024 // w
    extra = parted(total[:, :128], total[:, 128:], w)
    grads = jnp.concatenate([local_wqkv, local_wout], 1).astype(BF)
    for t in range(n):
        r, c = 16 * (t // across), w * (t % across)
        r0 = 16 * (t % ny)
        gout_ref[t // ny, r0 : r0 + 16, :] = grads[r : r + 16, c : c + w]
    for t in range(nx):
        gout_ref[t, 16 * ny :, :] = extra
    finish(sizes, *result)


def shards(sizes, features, valid, cotangent, gamma, w_qkv, w_out):
    n = sizes[0] * sizes[1]
    rows, width = features.shape
    assert rows == K
    block = rows // n
    root = float(rows * n) ** (-0.5)
    me = lax.axis_index("gx") * sizes[1] + lax.axis_index("gy")
    lane = jnp.arange(128, dtype=jnp.int32) // block
    spread = jnp.tile(valid.reshape(n, block), (1, 128 // block))
    spread = jnp.where(lane[None, :] == lax.rem(me, 128 // block), spread, 0).astype(F32)[:, None, :]

    vmem = pl.BlockSpec(memory_space=pltpu.VMEM)
    node = jax.ShapeDtypeStruct((rows, width), BF)
    tile = 16384 // n
    nx, ny = sizes
    y_plain, dx, grads = pl.pallas_call(
        functools.partial(patch_kernel, sizes),
        out_shape=(node, node, jax.ShapeDtypeStruct((nx, 16 * ny + 16, tile), BF)),
        in_specs=[vmem] * 6,
        out_specs=(vmem,) * 3,
        scratch_shapes=[
            pltpu.VMEM((K, width), BF),
            pltpu.VMEM((n, 1, 128), F32),
            pltpu.VMEM((K, width), BF),
            pltpu.VMEM((K, width), BF),
            pltpu.VMEM((HEADS, K, K), BF),
            pltpu.VMEM((width, K), F32),
            pltpu.VMEM((HEADS, 8, K), F32),
            pltpu.VMEM((3 * width, K), BF),
            pltpu.VMEM((width, K), BF),
            pltpu.VMEM((width, K), BF),
            pltpu.VMEM((3 * width, K), BF),
            pltpu.VMEM((K, width), BF),
            pltpu.VMEM((16, K), BF),
            pltpu.SemaphoreType.DMA((4, n)),
            pltpu.SemaphoreType.DMA((4, n)),
        ],
        compiler_params=pltpu.CompilerParams(collective_id=0, has_side_effects=True, vmem_limit_bytes=LIMIT),
        name="patch",
    )(features, spread, cotangent, gamma.reshape(1, width), w_qkv, w_out)

    dx_plain, gw, gwo, gg = pl.pallas_call(
        functools.partial(outward_kernel, sizes, root),
        out_shape=(
            node,
            jax.ShapeDtypeStruct((width, 3 * width), F32),
            jax.ShapeDtypeStruct((width, width), F32),
            jax.ShapeDtypeStruct((1, width), F32),
        ),
        in_specs=[vmem] * 2,
        out_specs=(vmem,) * 4,
        scratch_shapes=[
            pltpu.VMEM((nx, 16 * ny + 16, tile), BF),
            pltpu.VMEM((16 * ny + 16, tile), BF),
            pltpu.VMEM((ny, 16 * ny + 16, tile), BF),
            pltpu.VMEM((16 * ny, tile), BF),
            pltpu.VMEM((nx, 16 * ny, tile), BF),
            pltpu.SemaphoreType.DMA((n,)),
            pltpu.SemaphoreType.DMA((n,)),
        ] + [pltpu.SemaphoreType.DMA((size,)) for size in (nx, nx, ny, ny, nx, nx)],
        compiler_params=pltpu.CompilerParams(collective_id=1, has_side_effects=True, vmem_limit_bytes=LIMIT),
        name="outward",
    )(dx, grads)
    return y_plain, dx_plain, gw, gwo, gg.reshape(width)


def solution(mesh):
    sizes = (mesh.shape["gx"], mesh.shape["gy"])
    both = P(("gx", "gy"), None)
    return jax.shard_map(
        functools.partial(shards, sizes),
        mesh=mesh,
        in_specs=(both, P(("gx", "gy")), both, P(), P(), P()),
        out_specs=(both, both, P(), P(), P()),
        check_vma=False,
    )
```
